32 devices in a mesh: blk: 8 (over z, x), group: 4 (over y, core).
Axes of the slice: x: 2, y: 2, z: 4, core: 2. Of those that a mesh axis runs over, the one named last changes fastest.
Arguments:
- image_embed: float32 [8192, 768], P(('blk', 'group')), may hold values from -6 to 6
- text_embed: float32 [8192, 768], P(('blk', 'group')), may hold values from -6 to 6
- image_lse: float32 [8192], P(('blk', 'group')), as said below
- text_lse: float32 [8192], P(('blk', 'group')), as said below
Outputs:
- grad_image: float32 [8192, 768], P(('blk', 'group'))
- grad_text: float32 [8192, 768], P(('blk', 'group'))
The draws below stay inside these ranges and needn't reach their ends.
Inputs may be any that keep to these rules, and one draw needn't show every extreme that they name: `image_lse`: each value lies between c and c + 2, where c = 100 * sqrt(2 ln(1536) / 768). `text_lse`: each value lies between c and c + 2, where c = 100 * sqrt(2 ln(1536) / 768).
All inputs are finite; a program needn't handle non-finite values.
Results may differ from the reference program's by a relative error of at most 0.0003.
Values sent between devices are 32-bit elements; how exact they have to be, the bound alone decides.
A program may use at most 64 MiB of HBM per device.

```python
import math
import jax
import jax.numpy as jnp
from jax import lax

D = 768
ROWS_DEV = 256
STEPS = 3
PASSES = 2
BATCH = 8192
N_BLK = 8
N_GROUP = 4


def stat_values(key):
    spread = 100.0 / math.sqrt(D)
    center = spread * math.sqrt(2.0 * math.log(ROWS_DEV * PASSES * STEPS))
    return center + jax.random.uniform(key, (BATCH,), jnp.float32, 0.0, 2.0)


def draw_image_lse(key, part):
    key = jax.random.fold_in(key, 11)
    return stat_values(key)


def draw_text_lse(key, part):
    key = jax.random.fold_in(key, 23)
    return stat_values(key)


def block_levels(own_key, dims, cuts, low, high):
    def one(position, parts):
        draws = jax.random.uniform(jax.random.fold_in(jax.random.fold_in(own_key, 6), position), (parts,), jnp.float32, low / len(cuts), high / len(cuts))
        return jnp.repeat(jnp.exp(draws), dims[position] // parts).reshape((-1,) + (1,) * (len(dims) - position - 1))

    loudness = one(*cuts[0])
    for cut in cuts[1:]:
        loudness = loudness * one(*cut)
    return loudness


def scatter_about(key, dims, scale, bound, shards=(), kind=jnp.bfloat16):
    level = block_levels(key, dims, shards, -0.22, 0.18) if shards else 1.0
    drawn = jax.random.normal(key, dims, jnp.float32) * scale * level
    return jnp.minimum(jnp.maximum(drawn, -bound), bound).astype(kind)


def setup_inputs(seed: int = 0) -> dict:
    keys = jax.random.split(jax.random.key(seed), 5)
    return {
        "image_embed": scatter_about(keys[0], (BATCH, D), 1.0, 6.0, ((0, 32),), jnp.float32),
        "text_embed": scatter_about(keys[1], (BATCH, D), 1.0, 6.0, ((0, 32),), jnp.float32),
        "image_lse": draw_image_lse(jax.random.fold_in(keys[4], 71), 0),
        "text_lse": draw_text_lse(jax.random.fold_in(keys[4], 71), 0),
    }


logit_scale = 100.0
epsilon = 1e-06
highest = lax.Precision.HIGHEST

def unit_rows(raw):
    inverse = lax.rsqrt(lax.optimization_barrier(jnp.sum(raw * raw, axis=-1, keepdims=True)) + epsilon)
    return (raw * inverse, inverse)

def reference(image_embed, text_embed, image_lse, text_lse):
    blocked_shape = (N_BLK, N_GROUP, ROWS_DEV, D)
    image_unit, image_inverse = unit_rows(image_embed.reshape(blocked_shape))
    text_unit, text_inverse = unit_rows(text_embed.reshape(blocked_shape))
    image_stat = image_lse.reshape(N_BLK, N_GROUP, ROWS_DEV)
    text_stat = text_lse.reshape(N_BLK, N_GROUP, ROWS_DEV)
    identity = jnp.eye(ROWS_DEV, dtype=jnp.float32)
    grad_image_unit = jnp.zeros(blocked_shape, jnp.float32)
    grad_text_unit = jnp.zeros(blocked_shape, jnp.float32)
    for pass_index in range(PASSES):
        for cycle_step in range(STEPS):
            visiting = jnp.roll(text_unit, (cycle_step, pass_index), axis=(0, 1))
            visiting_stat = jnp.roll(text_stat, (cycle_step, pass_index), axis=(0, 1))
            scores = logit_scale * jnp.einsum('xgid,xgjd->xgij', image_unit, visiting, precision=highest)
            weight = 0.5 * (jnp.exp(scores - image_stat[..., :, None]) + jnp.exp(scores - visiting_stat[..., None, :]))
            if cycle_step == 0 and pass_index == 0:
                weight = weight - identity
            grad_image_unit = grad_image_unit + logit_scale * jnp.einsum('xgij,xgjd->xgid', weight, visiting, precision=highest)
            tile_text = logit_scale * jnp.einsum('xgij,xgid->xgjd', weight, image_unit, precision=highest)
            grad_text_unit = grad_text_unit + jnp.roll(tile_text, (-cycle_step, -pass_index), axis=(0, 1))
    grad_image = (grad_image_unit - image_unit * lax.optimization_barrier(jnp.sum(image_unit * grad_image_unit, axis=-1, keepdims=True))) * image_inverse
    grad_text = (grad_text_unit - text_unit * lax.optimization_barrier(jnp.sum(text_unit * grad_text_unit, axis=-1, keepdims=True))) * text_inverse
    return (grad_image.reshape(BATCH, D), grad_text.reshape(BATCH, D))
```

```python
import functools

import jax
import jax.numpy as jnp
from jax import lax
from jax.experimental import pallas as pl
from jax.experimental.pallas import tpu as pltpu
from jax.sharding import PartitionSpec as P

MESH = pl.DeviceIdType.MESH
CHUNKS = 4
OWN, MID, FAR = 0, 1, 2
TO_FAR, TO_MID, TO_IMAGE, BACK_FAR, BACK_MID, BACK_IMAGE = range(6)

logit_scale = 100.0
epsilon = 1e-06
NT = (((1,), (1,)), ((), ()))
NN = (((1,), (0,)), ((), ()))


def split(value):
    high = value.astype(jnp.bfloat16)
    return high, (value - high.astype(jnp.float32)).astype(jnp.bfloat16)


def dot_split(a, b, dims):
    dot = functools.partial(lax.dot_general, dimension_numbers=dims, preferred_element_type=jnp.float32)
    return dot(a[0], b[0]) + (dot(a[0], b[1]) + dot(a[1], b[0]))


def unit_rows(raw):
    inverse = lax.rsqrt(jnp.sum(raw * raw, axis=-1, keepdims=True) + epsilon)
    return raw * inverse, inverse


def project_back(grad_unit, raw):
    unit, inverse = unit_rows(raw)
    return (grad_unit - unit * jnp.sum(unit * grad_unit, axis=-1, keepdims=True)) * inverse


def kernel(
    n_blk, n_group,
    image_ref, text_ref, image_lse_ref, text_lse_ref, grad_image_ref, grad_text_ref,
    raw_far, raw_mid, raw_image, lse_far, lse_mid, lse_image,
    text_high, text_low, text_column, image_high, image_low, weights,
    g_own, g_far, g_mid, got_far, got_mid, g_image, got_image,
    send_sem, recv_sem,
):
    rows, width = image_ref.shape
    chunk = rows // CHUNKS
    blk, group = lax.axis_index("blk"), lax.axis_index("group")
    odd = lax.rem(blk, 2) == 1
    even = lax.rem(blk, 2) == 0
    ahead = (lax.rem(blk + 2, n_blk), group)
    behind = (lax.rem(blk + n_blk - 2, n_blk), group)
    partner = (blk + 1 - 2 * lax.rem(blk, 2), group)
    higher = (blk, lax.rem(group + 1, n_group))
    lower = (blk, lax.rem(group + n_group - 1, n_group))

    barrier = pltpu.get_barrier_semaphore()
    for device in (ahead, behind, partner, higher, lower):
        pl.semaphore_signal(barrier, inc=1, device_id=device, device_id_type=MESH)
    pl.semaphore_wait(barrier, 5)

    def part(k):
        return pl.ds(pl.multiple_of(k * chunk, chunk), chunk)

    def copy(src, dst, kind, slot, device):
        return pltpu.make_async_remote_copy(
            src_ref=src, dst_ref=dst, send_sem=send_sem.at[kind, slot], recv_sem=recv_sem.at[kind, slot],
            device_id=device, device_id_type=MESH,
        )

    def to_far(k):
        return copy(text_ref.at[part(k)], raw_far.at[part(k)], TO_FAR, k, ahead)

    def to_mid(k, source):
        return copy(source.at[part(k)], raw_mid.at[part(k)], TO_MID, k, partner)

    def lse_to_far():
        return copy(text_lse_ref, lse_far, TO_FAR, CHUNKS, ahead)

    def lse_to_mid(source):
        return copy(source, lse_mid, TO_MID, CHUNKS, partner)

    def to_image():
        return copy(image_ref, raw_image, TO_IMAGE, 0, lower)

    def lse_to_image():
        return copy(image_lse_ref, lse_image, TO_IMAGE, CHUNKS, lower)

    def back_far(k):
        return copy(g_far.at[part(k)], got_far.at[part(k)], BACK_FAR, k, behind)

    def back_mid(k):
        return copy(g_mid.at[part(k)], got_mid.at[part(k)], BACK_MID, k, partner)

    def back_image():
        return copy(g_image.at[pl.ds(rows, rows)], got_image, BACK_IMAGE, 0, higher)

    lse_to_far().start()
    lse_to_image().start()

    @pl.when(even)
    def _():
        lse_to_mid(text_lse_ref).start()

    for k in range(CHUNKS):
        to_far(k).start()

        @pl.when(even)
        def _():
            to_mid(k, text_ref).start()

        if k == 0:
            to_image().start()

    def take_text(which, raw, k):
        unit, _ = unit_rows(raw[part(k), :])
        text_high[which, part(k), :], text_low[which, part(k), :] = split(unit)

    def take_column(which, lse):
        text_column[which] = jnp.transpose(jnp.broadcast_to(lse[...], (128, rows)))

    def take_image(first, raw):
        @pl.loop(0, CHUNKS)
        def _(k):
            unit, _ = unit_rows(raw[part(k), :])
            here = pl.ds(pl.multiple_of(first + k * chunk, chunk), chunk)
            image_high[here, :], image_low[here, :] = split(unit)

    def tile(which, k, columns, lse, diagonal=False):
        text = (text_high[which, part(k), :], text_low[which, part(k), :])
        image = (image_high[columns, :], image_low[columns, :])
        scores = logit_scale * dot_split(text, image, NT)
        weight = (0.5 * logit_scale) * (
            jnp.exp(scores - lse) + jnp.exp(scores - text_column[which, part(k), 0:1])
        )
        if diagonal:
            row = lax.broadcasted_iota(jnp.int32, weight.shape, 0) + k * chunk
            column = lax.broadcasted_iota(jnp.int32, weight.shape, 1)
            weight = weight - jnp.where(row == column, logit_scale, 0.0)
        weights[which, part(k), columns] = weight
        return dot_split(split(weight), image, NN)

    first, second, both = pl.ds(0, rows), pl.ds(rows, rows), pl.ds(0, 2 * rows)

    def image_grad(which, half):
        weight = split(jnp.transpose(weights[which, :, half]))
        return dot_split(weight, (text_high[which], text_low[which]), NN)

    take_column(OWN, text_lse_ref)
    take_image(0, image_ref)

    @pl.loop(0, CHUNKS)
    def _(k):
        take_text(OWN, text_ref, k)
        g_own[part(k), :] = tile(OWN, k, first, image_lse_ref[...], diagonal=True)

    lse_to_far().wait_recv()

    @pl.when(odd)
    def _():
        lse_to_mid(lse_far).start()

    take_column(FAR, lse_far)

    def receive_far(k):
        to_far(k).wait_recv()

        @pl.when(odd)
        def _():
            to_mid(k, raw_far).start()

    receive_far(0)
    receive_far(1)
    lse_to_image().wait_recv()
    to_image().wait_recv()
    take_image(rows, raw_image)

    @pl.loop(0, CHUNKS)
    def _(k):
        g_own[part(k), :] += tile(OWN, k, second, lse_image[...])

    lse_to_mid(text_lse_ref).wait_recv()
    take_column(MID, lse_mid)
    both_lse = jnp.concatenate([image_lse_ref[...], lse_image[...]], axis=1)

    def pass_on(k):
        back_mid(k).wait_recv()
        g_far[part(k), :] += got_mid[part(k), :]
        back_far(k).start()

    @pl.loop(0, CHUNKS + 1)
    def _(k):
        @pl.when(k < CHUNKS)
        def _():
            take_text(FAR, raw_far, k)
            g_far[part(k), :] = tile(FAR, k, both, both_lse)

            @pl.when(even)
            def _():
                back_far(k).start()

        @pl.when(k + 2 < CHUNKS)
        def _():
            receive_far(k + 2)

        @pl.when(k > 0)
        def _():
            to_mid(k - 1, text_ref).wait_recv()
            take_text(MID, raw_mid, k - 1)
            g_mid[part(k - 1), :] = tile(MID, k - 1, both, both_lse)
            back_mid(k - 1).start()

        @pl.when(jnp.logical_and(odd, k > 1))
        def _():
            pass_on(k - 2)

    g_image[second, :] = image_grad(OWN, second) + image_grad(MID, second) + image_grad(FAR, second)
    back_image().start()

    @pl.when(odd)
    def _():
        pass_on(CHUNKS - 1)

    g_image[first, :] = image_grad(OWN, first) + image_grad(MID, first) + image_grad(FAR, first)
    back_image().wait_recv()

    @pl.loop(0, CHUNKS)
    def _(k):
        grad_image_ref[part(k), :] = project_back(
            g_image[part(k), :] + got_image[part(k), :], image_ref[part(k), :]
        )

    @pl.loop(0, CHUNKS)
    def _(k):
        @pl.when(even)
        def _():
            back_mid(k).wait_recv()
            g_own[part(k), :] += got_mid[part(k), :]

        back_far(k).wait_recv()
        grad_text_ref[part(k), :] = project_back(
            g_own[part(k), :] + got_far[part(k), :], text_ref[part(k), :]
        )

    lse_to_far().wait_send()
    lse_to_mid(text_lse_ref).wait_send()
    lse_to_image().wait_send()
    to_image().wait_send()
    back_image().wait_send()

    @pl.loop(0, CHUNKS)
    def _(k):
        to_far(k).wait_send()
        to_mid(k, text_ref).wait_send()
        back_far(k).wait_send()
        back_mid(k).wait_send()


def solution(mesh):
    n_blk, n_group = mesh.shape["blk"], mesh.shape["group"]

    def per_device(image_embed, text_embed, image_lse, text_lse):
        rows, width = image_embed.shape
        block = jax.ShapeDtypeStruct((rows, width), jnp.float32)
        whole = pltpu.VMEM((rows, width), jnp.float32)
        line = pltpu.VMEM((1, rows), jnp.float32)
        return pl.pallas_call(
            functools.partial(kernel, n_blk, n_group),
            out_shape=(block, block),
            in_specs=[pl.BlockSpec(memory_space=pltpu.VMEM)] * 4,
            out_specs=[pl.BlockSpec(memory_space=pltpu.VMEM)] * 2,
            scratch_shapes=[
                whole, whole, whole, line, line, line,
                pltpu.VMEM((3, rows, width), jnp.bfloat16),
                pltpu.VMEM((3, rows, width), jnp.bfloat16),
                pltpu.VMEM((3, rows, 128), jnp.float32),
                pltpu.VMEM((2 * rows, width), jnp.bfloat16),
                pltpu.VMEM((2 * rows, width), jnp.bfloat16),
                pltpu.VMEM((3, rows, 2 * rows), jnp.float32),
                whole, whole, whole, whole, whole,
                pltpu.VMEM((2 * rows, width), jnp.float32),
                whole,
                pltpu.SemaphoreType.DMA((6, CHUNKS + 1)),
                pltpu.SemaphoreType.DMA((6, CHUNKS + 1)),
            ],
            compiler_params=pltpu.CompilerParams(
                collective_id=0, has_side_effects=True, vmem_limit_bytes=40 * 1024 * 1024
            ),
        )(image_embed, text_embed, image_lse.reshape(1, rows), text_lse.reshape(1, rows))

    spec = P(("blk", "group"), None)
    line = P(("blk", "group"))
    return jax.shard_map(
        per_device, mesh=mesh, in_specs=(spec, spec, line, line), out_specs=(spec, spec), check_vma=False
    )
```

```python
import functools

import jax
import jax.numpy as jnp
from jax import lax
from jax.experimental import pallas as pl
from jax.experimental.pallas import tpu as pltpu
from jax.sharding import PartitionSpec as P

MESH = pl.DeviceIdType.MESH
CHUNKS = 4
PIECES = 8
DIRECT = 0
OWN, MID, FAR = 0, 1, 2
TO_FAR, TO_MID, TO_IMAGE, BACK_FAR, BACK_MID, BACK_IMAGE = range(6)

logit_scale = 100.0
epsilon = 1e-06
NT = (((1,), (1,)), ((), ()))
NN = (((1,), (0,)), ((), ()))


def split(value):
    high = value.astype(jnp.bfloat16)
    return high, (value - high.astype(jnp.float32)).astype(jnp.bfloat16)


def dot_split(a, b, dims):
    dot = functools.partial(lax.dot_general, dimension_numbers=dims, preferred_element_type=jnp.float32)
    rows = a[0].shape[0]
    by_high = dot(jnp.concatenate(a, axis=0), b[0])
    return by_high[:rows] + (by_high[rows:] + dot(a[0], b[1]))


def unit_rows(raw):
    inverse = lax.rsqrt(jnp.sum(raw * raw, axis=-1, keepdims=True) + epsilon)
    return raw * inverse, inverse


def project_back(grad_unit, raw):
    unit, inverse = unit_rows(raw)
    return (grad_unit - unit * jnp.sum(unit * grad_unit, axis=-1, keepdims=True)) * inverse


def kernel(
    n_blk, n_group,
    image_hbm, text_hbm, image_lse_hbm, text_lse_hbm, grad_image_hbm, grad_text_hbm,
    image_ref, text_ref, image_lse_ref, text_lse_ref, load_sem,
    grad_image_ref, grad_text_ref, store_sem,
    raw_far, raw_mid, raw_image, lse_far, lse_mid, lse_image,
    text_high, text_low, text_column, image_high, image_low, weights,
    g_own, g_far, g_mid, got_far, got_mid, g_image, got_image,
    send_sem, recv_sem,
):
    rows, width = image_ref.shape
    chunk = rows // CHUNKS
    blk, group = lax.axis_index("blk"), lax.axis_index("group")
    odd = lax.rem(blk, 2) == 1
    even = lax.rem(blk, 2) == 0
    ahead = (lax.rem(blk + 2, n_blk), group)
    behind = (lax.rem(blk + n_blk - 2, n_blk), group)
    partner = (blk + 1 - 2 * lax.rem(blk, 2), group)
    onward = (lax.rem(blk + 1, n_blk), group)
    diagonal = (lax.rem(blk + n_blk - 1 + 2 * lax.rem(blk, 2), n_blk), group)
    higher = (blk, lax.rem(group + 1, n_group))
    lower = (blk, lax.rem(group + n_group - 1, n_group))

    load_text = pltpu.make_async_copy(text_hbm, text_ref, load_sem.at[0])
    load_image = pltpu.make_async_copy(image_hbm, image_ref, load_sem.at[1])
    load_text_lse = pltpu.make_async_copy(text_lse_hbm, text_lse_ref, load_sem.at[2])
    load_image_lse = pltpu.make_async_copy(image_lse_hbm, image_lse_ref, load_sem.at[3])
    for load in (load_image, load_text, load_text_lse, load_image_lse):
        load.start()

    barrier = pltpu.get_barrier_semaphore()
    for device in (ahead, behind, partner, diagonal, higher, lower):
        pl.semaphore_signal(barrier, inc=1, device_id=device, device_id_type=MESH)
    pl.semaphore_wait(barrier, 6)

    def part(k):
        return pl.ds(pl.multiple_of(k * chunk, chunk), chunk)

    def piece(j):
        size = rows // PIECES
        return pl.ds(pl.multiple_of(j * size, size), size)

    def copy(src, dst, kind, slot, device):
        return pltpu.make_async_remote_copy(
            src_ref=src, dst_ref=dst, send_sem=send_sem.at[kind, slot], recv_sem=recv_sem.at[kind, slot],
            device_id=device, device_id_type=MESH,
        )

    def to_far(k):
        return copy(text_hbm.at[piece(k)], raw_far.at[piece(k)], TO_FAR, k, ahead)

    def to_mid(k, source):
        return copy(source.at[piece(k)], raw_mid.at[piece(k)], TO_MID, k, partner)

    def store_image(k):
        return pltpu.make_async_copy(grad_image_ref.at[part(k)], grad_image_hbm.at[part(k)], store_sem.at[0, k])

    def store_text(k):
        return pltpu.make_async_copy(grad_text_ref.at[part(k)], grad_text_hbm.at[part(k)], store_sem.at[1, k])

    def lse_to_far():
        return copy(text_lse_hbm, lse_far, TO_FAR, PIECES, ahead)

    def to_mid_direct(j):
        return copy(text_hbm.at[piece(j)], raw_mid.at[piece(j)], TO_MID, j, onward)

    def lse_to_mid():
        return copy(text_lse_hbm, lse_mid, TO_MID, PIECES, onward)

    def to_image():
        return copy(image_hbm, raw_image, TO_IMAGE, 0, lower)

    def lse_to_image():
        return copy(image_lse_hbm, lse_image, TO_IMAGE, PIECES, lower)

    def back_far(k):
        return copy(g_far.at[piece(k)], got_far.at[piece(k)], BACK_FAR, k, behind)

    def back_mid(k):
        return copy(g_mid.at[piece(k)], got_mid.at[piece(k)], BACK_MID, k, partner)

    def back_image():
        return copy(g_image.at[pl.ds(rows, rows)], got_image, BACK_IMAGE, 0, higher)

    lse_to_far().start()
    lse_to_mid().start()
    lse_to_image().start()
    for j in range(DIRECT):
        to_mid_direct(j).start()
    for j in range(PIECES):
        to_far(j).start()

        if j >= DIRECT:
            @pl.when(even)
            def _():
                to_mid(j, text_hbm).start()

        if j == 0:
            to_image().start()

    def take_text(which, raw, k):
        unit, _ = unit_rows(raw[part(k), :])
        text_high[which, part(k), :], text_low[which, part(k), :] = split(unit)

    def take_column(which, lse):
        text_column[which] = jnp.transpose(jnp.broadcast_to(lse[...], (128, rows)))

    def take_image(first, raw):
        @pl.loop(0, CHUNKS)
        def _(k):
            unit, _ = unit_rows(raw[part(k), :])
            here = pl.ds(pl.multiple_of(first + k * chunk, chunk), chunk)
            image_high[here, :], image_low[here, :] = split(unit)

    def tile(which, here, columns, lse, diagonal=False):
        text = (text_high[which, here, :], text_low[which, here, :])
        image = (image_high[columns, :], image_low[columns, :])
        scores = logit_scale * dot_split(text, image, NT)
        weight = (0.5 * logit_scale) * (
            jnp.exp(scores - lse) + jnp.exp(scores - text_column[which, here, 0:1])
        )
        if diagonal:
            row = lax.broadcasted_iota(jnp.int32, weight.shape, 0)
            column = lax.broadcasted_iota(jnp.int32, weight.shape, 1)
            weight = weight - jnp.where(row == column, logit_scale, 0.0)
        weights[which, here, columns] = weight
        return dot_split(split(weight), image, NN)

    first, second, both = pl.ds(0, rows), pl.ds(rows, rows), pl.ds(0, 2 * rows)

    def image_grad(half):
        turned = jnp.concatenate([jnp.transpose(weights[which, :, half]) for which in range(3)], axis=1)
        texts = [ref[...].reshape(3 * rows, width) for ref in (text_high, text_low)]
        return dot_split(split(turned), texts, NN)

    load_image.wait()
    take_image(0, image_ref)
    load_text_lse.wait()
    load_image_lse.wait()
    take_column(OWN, text_lse_ref)
    load_text.wait()

    @pl.loop(0, CHUNKS)
    def _(k):
        take_text(OWN, text_ref, k)

    g_own[...] = tile(OWN, first, first, image_lse_ref[...], diagonal=True)

    lse_to_far().wait_recv()

    take_column(FAR, lse_far)

    def receive_far(j):
        @pl.when(odd)
        def _():
            to_far(j).wait_recv()
            if isinstance(j, int) and j < DIRECT:
                return
            to_mid(j, raw_far).start()

    for j in range(PIECES // 2):
        receive_far(j)
    lse_to_image().wait_recv()
    to_image().wait_recv()
    take_image(rows, raw_image)

    g_own[...] += tile(OWN, first, second, lse_image[...])

    lse_to_mid().wait_recv()
    take_column(MID, lse_mid)
    both_lse = jnp.concatenate([image_lse_ref[...], lse_image[...]], axis=1)

    def pass_on(j):
        @pl.when(odd)
        def _():
            back_mid(j).wait_recv()
            g_far[piece(j), :] += got_mid[piece(j), :]
            back_far(j).start()

    half = PIECES // 2
    per = PIECES // CHUNKS

    @pl.loop(0, CHUNKS)
    def _(k):
        late = k >= CHUNKS // 2
        early = k < CHUNKS // 2

        @pl.when(late)
        def _():
            pass_on(2 * k - half)

        for j in range(per):
            to_mid(per * k + j, text_hbm).wait_recv()
        take_text(MID, raw_mid, k)
        g_mid[part(k), :] = tile(MID, part(k), both, both_lse)

        @pl.when(jnp.logical_or(even, late))
        def _():
            for j in range(per):
                back_mid(per * k + j).start()

        @pl.when(early)
        def _():
            receive_far(half + 2 * k)

        @pl.when(late)
        def _():
            pass_on(2 * k + 1 - half)

        @pl.when(even)
        def _():
            for j in range(per):
                to_far(per * k + j).wait_recv()

        take_text(FAR, raw_far, k)
        g_far[part(k), :] = tile(FAR, part(k), both, both_lse)

        @pl.when(even)
        def _():
            for j in range(per):
                back_far(per * k + j).start()

        @pl.when(early)
        def _():
            receive_far(half + 2 * k + 1)

        @pl.when(jnp.logical_and(odd, k == CHUNKS // 2 - 1))
        def _():
            for j in range(half):
                back_mid(j).start()

    pass_on(half)
    g_image[second, :] = image_grad(second)
    back_image().start()
    pass_on(half + 1)
    g_image[first, :] = image_grad(first)
    pass_on(half + 2)
    pass_on(half + 3)
    back_image().wait_recv()

    @pl.loop(0, CHUNKS)
    def _(k):
        grad_image_ref[part(k), :] = project_back(
            g_image[part(k), :] + got_image[part(k), :], image_ref[part(k), :]
        )
        store_image(k).start()

    @pl.loop(0, CHUNKS)
    def _(k):
        @pl.when(even)
        def _():
            for j in range(per):
                back_mid(per * k + j).wait_recv()
            g_own[part(k), :] += got_mid[part(k), :]

        for j in range(per):
            back_far(per * k + j).wait_recv()
        grad_text_ref[part(k), :] = project_back(
            g_own[part(k), :] + got_far[part(k), :], text_ref[part(k), :]
        )
        store_text(k).start()

    lse_to_far().wait_send()
    lse_to_mid().wait_send()
    lse_to_image().wait_send()
    to_image().wait_send()
    back_image().wait_send()

    @pl.loop(0, PIECES)
    def _(k):
        to_far(k).wait_send()
        to_mid(k, text_hbm).wait_send()
        back_far(k).wait_send()
        back_mid(k).wait_send()

    @pl.loop(0, CHUNKS)
    def _(k):
        store_image(k).wait()
        store_text(k).wait()


def solution(mesh):
    n_blk, n_group = mesh.shape["blk"], mesh.shape["group"]

    def per_device(image_embed, text_embed, image_lse, text_lse):
        rows, width = image_embed.shape
        block = jax.ShapeDtypeStruct((rows, width), jnp.float32)
        whole = pltpu.VMEM((rows, width), jnp.float32)
        line = pltpu.VMEM((1, rows), jnp.float32)
        grads = pl.pallas_call(
            functools.partial(kernel, n_blk, n_group),
            out_shape=(block, block),
            in_specs=[pl.BlockSpec(memory_space=pl.ANY)] * 4,
            out_specs=[pl.BlockSpec(memory_space=pl.ANY)] * 2,
            scratch_shapes=[
                whole, whole, line, line, pltpu.SemaphoreType.DMA((4,)),
                whole, whole, pltpu.SemaphoreType.DMA((2, CHUNKS)),
                whole, whole, whole, line, line, line,
                pltpu.VMEM((3, rows, width), jnp.bfloat16),
                pltpu.VMEM((3, rows, width), jnp.bfloat16),
                pltpu.VMEM((3, rows, 128), jnp.float32),
                pltpu.VMEM((2 * rows, width), jnp.bfloat16),
                pltpu.VMEM((2 * rows, width), jnp.bfloat16),
                pltpu.VMEM((3, rows, 2 * rows), jnp.float32),
                whole, whole, whole, whole, whole,
                pltpu.VMEM((2 * rows, width), jnp.float32),
                whole,
                pltpu.SemaphoreType.DMA((6, PIECES + 1)),
                pltpu.SemaphoreType.DMA((6, PIECES + 1)),
            ],
            compiler_params=pltpu.CompilerParams(
                collective_id=0, has_side_effects=True, vmem_limit_bytes=62 * 1024 * 1024
            ),
        )(image_embed, text_embed, image_lse.reshape(1, rows), text_lse.reshape(1, rows))
        return grads

    spec = P(("blk", "group"), None)
    line = P(("blk", "group"))
    return jax.shard_map(
        per_device, mesh=mesh, in_specs=(spec, spec, line, line), out_specs=(spec, spec), check_vma=False
    )
```

```python
import functools

import jax
import jax.numpy as jnp
from jax import lax
from jax.experimental import pallas as pl
from jax.experimental.pallas import tpu as pltpu
from jax.sharding import PartitionSpec as P

MESH = pl.DeviceIdType.MESH
CHUNKS = 4
PIECES = 8
DIRECT = 0
OWN, MID, FAR = 0, 1, 2
TO_FAR, TO_MID, TO_IMAGE, BACK_FAR, BACK_MID, BACK_IMAGE = range(6)

logit_scale = 100.0
epsilon = 1e-06
NT = (((1,), (1,)), ((), ()))
NN = (((1,), (0,)), ((), ()))


def split(value):
    high = value.astype(jnp.bfloat16)
    return high, (value - high.astype(jnp.float32)).astype(jnp.bfloat16)


def dot_split(a, b, dims):
    dot = functools.partial(lax.dot_general, dimension_numbers=dims, preferred_element_type=jnp.float32)
    rows = a[0].shape[0]
    by_high = dot(jnp.concatenate(a, axis=0), b[0])
    return by_high[:rows] + (by_high[rows:] + dot(a[0], b[1]))


def unit_rows(raw):
    inverse = lax.rsqrt(jnp.sum(raw * raw, axis=-1, keepdims=True) + epsilon)
    return raw * inverse, inverse


def project_back(grad_unit, raw):
    unit, inverse = unit_rows(raw)
    return (grad_unit - unit * jnp.sum(unit * grad_unit, axis=-1, keepdims=True)) * inverse


def kernel(
    n_blk, n_group,
    image_hbm, text_hbm, image_lse_hbm, text_lse_hbm, grad_image_ref, grad_text_ref,
    image_ref, text_ref, image_lse_ref, text_lse_ref, load_sem,
    raw_far, raw_mid, raw_image, lse_far, lse_mid, lse_image,
    text_high, text_low, text_column, image_high, image_low, weights,
    g_own, g_far, g_mid, got_far, got_mid, g_image, got_image,
    send_sem, recv_sem,
):
    rows, width = image_ref.shape
    chunk = rows // CHUNKS
    blk, group = lax.axis_index("blk"), lax.axis_index("group")
    odd = lax.rem(blk, 2) == 1
    even = lax.rem(blk, 2) == 0
    ahead = (lax.rem(blk + 2, n_blk), group)
    behind = (lax.rem(blk + n_blk - 2, n_blk), group)
    partner = (blk + 1 - 2 * lax.rem(blk, 2), group)
    onward = (lax.rem(blk + 1, n_blk), group)
    diagonal = (lax.rem(blk + n_blk - 1 + 2 * lax.rem(blk, 2), n_blk), group)
    higher = (blk, lax.rem(group + 1, n_group))
    lower = (blk, lax.rem(group + n_group - 1, n_group))

    load_text = pltpu.make_async_copy(text_hbm, text_ref, load_sem.at[0])
    load_image = pltpu.make_async_copy(image_hbm, image_ref, load_sem.at[1])
    load_text_lse = pltpu.make_async_copy(text_lse_hbm, text_lse_ref, load_sem.at[2])
    load_image_lse = pltpu.make_async_copy(image_lse_hbm, image_lse_ref, load_sem.at[3])
    for load in (load_image, load_text, load_text_lse, load_image_lse):
        load.start()

    barrier = pltpu.get_barrier_semaphore()
    for device in (ahead, behind, partner, diagonal, higher, lower):
        pl.semaphore_signal(barrier, inc=1, device_id=device, device_id_type=MESH)
    pl.semaphore_wait(barrier, 6)

    def part(k):
        return pl.ds(pl.multiple_of(k * chunk, chunk), chunk)

    def piece(j):
        size = rows // PIECES
        return pl.ds(pl.multiple_of(j * size, size), size)

    def copy(src, dst, kind, slot, device):
        return pltpu.make_async_remote_copy(
            src_ref=src, dst_ref=dst, send_sem=send_sem.at[kind, slot], recv_sem=recv_sem.at[kind, slot],
            device_id=device, device_id_type=MESH,
        )

    def to_far(k):
        return copy(text_hbm.at[piece(k)], raw_far.at[piece(k)], TO_FAR, k, ahead)

    def to_mid(k, source):
        return copy(source.at[piece(k)], raw_mid.at[piece(k)], TO_MID, k, partner)

    def lse_to_far():
        return copy(text_lse_hbm, lse_far, TO_FAR, PIECES, ahead)

    def to_mid_direct(j):
        return copy(text_hbm.at[piece(j)], raw_mid.at[piece(j)], TO_MID, j, onward)

    def lse_to_mid():
        return copy(text_lse_hbm, lse_mid, TO_MID, PIECES, onward)

    def to_image():
        return copy(image_hbm, raw_image, TO_IMAGE, 0, lower)

    def lse_to_image():
        return copy(image_lse_hbm, lse_image, TO_IMAGE, PIECES, lower)

    def back_far(k):
        return copy(g_far.at[piece(k)], got_far.at[piece(k)], BACK_FAR, k, behind)

    def back_mid(k):
        return copy(g_mid.at[piece(k)], got_mid.at[piece(k)], BACK_MID, k, partner)

    def back_image():
        return copy(g_image.at[pl.ds(rows, rows)], got_image, BACK_IMAGE, 0, higher)

    lse_to_far().start()
    lse_to_mid().start()
    lse_to_image().start()
    for j in range(DIRECT):
        to_mid_direct(j).start()
    for j in range(PIECES):
        to_far(j).start()

        if j >= DIRECT:
            @pl.when(even)
            def _():
                to_mid(j, text_hbm).start()

        if j == 0:
            to_image().start()

    def take_text(which, raw, k):
        unit, _ = unit_rows(raw[part(k), :])
        text_high[which, part(k), :], text_low[which, part(k), :] = split(unit)

    def take_column(which, lse):
        text_column[which] = jnp.transpose(jnp.broadcast_to(lse[...], (128, rows)))

    def take_image(first, raw):
        @pl.loop(0, CHUNKS)
        def _(k):
            unit, _ = unit_rows(raw[part(k), :])
            here = pl.ds(pl.multiple_of(first + k * chunk, chunk), chunk)
            image_high[here, :], image_low[here, :] = split(unit)

    def tile(which, here, columns, lse, diagonal=False):
        text = (text_high[which, here, :], text_low[which, here, :])
        image = (image_high[columns, :], image_low[columns, :])
        scores = logit_scale * dot_split(text, image, NT)
        weight = (0.5 * logit_scale) * (
            jnp.exp(scores - lse) + jnp.exp(scores - text_column[which, here, 0:1])
        )
        if diagonal:
            row = lax.broadcasted_iota(jnp.int32, weight.shape, 0)
            column = lax.broadcasted_iota(jnp.int32, weight.shape, 1)
            weight = weight - jnp.where(row == column, logit_scale, 0.0)
        weights[which, here, columns] = weight
        return dot_split(split(weight), image, NN)

    first, second, both = pl.ds(0, rows), pl.ds(rows, rows), pl.ds(0, 2 * rows)

    def image_grad(half):
        turned = jnp.concatenate([jnp.transpose(weights[which, :, half]) for which in range(3)], axis=1)
        texts = [ref[...].reshape(3 * rows, width) for ref in (text_high, text_low)]
        return dot_split(split(turned), texts, NN)

    load_image.wait()
    take_image(0, image_ref)
    load_text_lse.wait()
    load_image_lse.wait()
    take_column(OWN, text_lse_ref)
    load_text.wait()

    @pl.loop(0, CHUNKS)
    def _(k):
        take_text(OWN, text_ref, k)

    g_own[...] = tile(OWN, first, first, image_lse_ref[...], diagonal=True)

    lse_to_far().wait_recv()

    take_column(FAR, lse_far)

    def receive_far(j):
        @pl.when(odd)
        def _():
            to_far(j).wait_recv()
            if isinstance(j, int) and j < DIRECT:
                return
            to_mid(j, raw_far).start()

    for j in range(PIECES // 2):
        receive_far(j)
    lse_to_image().wait_recv()
    to_image().wait_recv()
    take_image(rows, raw_image)

    g_own[...] += tile(OWN, first, second, lse_image[...])

    lse_to_mid().wait_recv()
    take_column(MID, lse_mid)
    both_lse = jnp.concatenate([image_lse_ref[...], lse_image[...]], axis=1)

    def pass_on(j):
        @pl.when(odd)
        def _():
            back_mid(j).wait_recv()
            g_far[piece(j), :] += got_mid[piece(j), :]
            back_far(j).start()

    half = PIECES // 2
    per = PIECES // CHUNKS

    @pl.loop(0, CHUNKS)
    def _(k):
        late = k >= CHUNKS // 2
        early = k < CHUNKS // 2

        @pl.when(late)
        def _():
            pass_on(2 * k - half)

        for j in range(per):
            to_mid(per * k + j, text_hbm).wait_recv()
        take_text(MID, raw_mid, k)
        g_mid[part(k), :] = tile(MID, part(k), both, both_lse)

        @pl.when(jnp.logical_or(even, late))
        def _():
            for j in range(per):
                back_mid(per * k + j).start()

        @pl.when(early)
        def _():
            receive_far(half + 2 * k)

        @pl.when(late)
        def _():
            pass_on(2 * k + 1 - half)

        @pl.when(even)
        def _():
            for j in range(per):
                to_far(per * k + j).wait_recv()

        take_text(FAR, raw_far, k)
        g_far[part(k), :] = tile(FAR, part(k), both, both_lse)

        @pl.when(even)
        def _():
            for j in range(per):
                back_far(per * k + j).start()

        @pl.when(early)
        def _():
            receive_far(half + 2 * k + 1)

        @pl.when(jnp.logical_and(odd, k == CHUNKS // 2 - 1))
        def _():
            for j in range(half):
                back_mid(j).start()

    pass_on(half)
    g_image[second, :] = image_grad(second)
    back_image().start()
    pass_on(half + 1)
    g_image[first, :] = image_grad(first)
    pass_on(half + 2)
    pass_on(half + 3)
    back_image().wait_recv()

    @pl.loop(0, CHUNKS)
    def _(k):
        grad_image_ref[part(k), :] = project_back(
            g_image[part(k), :] + got_image[part(k), :], image_ref[part(k), :]
        )

    @pl.loop(0, CHUNKS)
    def _(k):
        @pl.when(even)
        def _():
            for j in range(per):
                back_mid(per * k + j).wait_recv()
            g_own[part(k), :] += got_mid[part(k), :]

        for j in range(per):
            back_far(per * k + j).wait_recv()
        grad_text_ref[part(k), :] = project_back(
            g_own[part(k), :] + got_far[part(k), :], text_ref[part(k), :]
        )

    lse_to_far().wait_send()
    lse_to_mid().wait_send()
    lse_to_image().wait_send()
    to_image().wait_send()
    back_image().wait_send()

    @pl.loop(0, PIECES)
    def _(k):
        to_far(k).wait_send()
        to_mid(k, text_hbm).wait_send()
        back_far(k).wait_send()
        back_mid(k).wait_send()


def solution(mesh):
    n_blk, n_group = mesh.shape["blk"], mesh.shape["group"]

    def per_device(image_embed, text_embed, image_lse, text_lse):
        rows, width = image_embed.shape
        block = jax.ShapeDtypeStruct((rows, width), jnp.float32)
        whole = pltpu.VMEM((rows, width), jnp.float32)
        line = pltpu.VMEM((1, rows), jnp.float32)
        grads = pl.pallas_call(
            functools.partial(kernel, n_blk, n_group),
            out_shape=(whole, whole),
            in_specs=[pl.BlockSpec(memory_space=pl.ANY)] * 4,
            out_specs=[pl.BlockSpec(memory_space=pltpu.VMEM)] * 2,
            scratch_shapes=[
                whole, whole, line, line, pltpu.SemaphoreType.DMA((4,)),
                whole, whole, whole, line, line, line,
                pltpu.VMEM((3, rows, width), jnp.bfloat16),
                pltpu.VMEM((3, rows, width), jnp.bfloat16),
                pltpu.VMEM((3, rows, 128), jnp.float32),
                pltpu.VMEM((2 * rows, width), jnp.bfloat16),
                pltpu.VMEM((2 * rows, width), jnp.bfloat16),
                pltpu.VMEM((3, rows, 2 * rows), jnp.float32),
                whole, whole, whole, whole, whole,
                pltpu.VMEM((2 * rows, width), jnp.float32),
                whole,
                pltpu.SemaphoreType.DMA((6, PIECES + 1)),
                pltpu.SemaphoreType.DMA((6, PIECES + 1)),
            ],
            compiler_params=pltpu.CompilerParams(
                collective_id=0, has_side_effects=True, vmem_limit_bytes=62 * 1024 * 1024
            ),
        )(image_embed, text_embed, image_lse.reshape(1, rows), text_lse.reshape(1, rows))
        return grads

    spec = P(("blk", "group"), None)
    line = P(("blk", "group"))
    return jax.shard_map(
        per_device, mesh=mesh, in_specs=(spec, spec, line, line), out_specs=(spec, spec), check_vma=False
    )
```

```python
import functools

import jax
import jax.numpy as jnp
from jax import lax
from jax.experimental import pallas as pl
from jax.experimental.pallas import tpu as pltpu
from jax.sharding import PartitionSpec as P

MESH = pl.DeviceIdType.MESH
CHUNKS = 4
PIECES = 8
DIRECT = 0
OWN, MID, FAR = 0, 1, 2
TO_FAR, TO_MID, TO_IMAGE, BACK_FAR, BACK_MID, BACK_IMAGE = range(6)

logit_scale = 100.0
epsilon = 1e-06
NT = (((1,), (1,)), ((), ()))
NN = (((1,), (0,)), ((), ()))


def split(value):
    high = value.astype(jnp.bfloat16)
    return high, (value - high.astype(jnp.float32)).astype(jnp.bfloat16)


def dot_split(a, b, dims):
    dot = functools.partial(lax.dot_general, dimension_numbers=dims, preferred_element_type=jnp.float32)
    rows = a[0].shape[0]
    by_high = dot(jnp.concatenate(a, axis=0), b[0])
    return by_high[:rows] + (by_high[rows:] + dot(a[0], b[1]))


def unit_rows(raw):
    inverse = lax.rsqrt(jnp.sum(raw * raw, axis=-1, keepdims=True) + epsilon)
    return raw * inverse, inverse


def project_back(grad_unit, raw):
    unit, inverse = unit_rows(raw)
    return (grad_unit - unit * jnp.sum(unit * grad_unit, axis=-1, keepdims=True)) * inverse


def kernel(
    n_blk, n_group,
    image_hbm, text_hbm, image_lse_hbm, text_lse_hbm, grad_image_ref, grad_text_ref,
    image_ref, text_ref, image_lse_ref, text_lse_ref, load_sem,
    raw_far, raw_mid, raw_image, lse_far, lse_mid, lse_image,
    text_high, text_low, text_column, image_high, image_low, weights,
    g_own, g_far, g_mid, got_far, got_mid, g_image, got_image,
    send_sem, recv_sem,
):
    rows, width = image_ref.shape
    chunk = rows // CHUNKS
    blk, group = lax.axis_index("blk"), lax.axis_index("group")
    odd = lax.rem(blk, 2) == 1
    even = lax.rem(blk, 2) == 0
    ahead = (lax.rem(blk + 2, n_blk), group)
    behind = (lax.rem(blk + n_blk - 2, n_blk), group)
    partner = (blk + 1 - 2 * lax.rem(blk, 2), group)
    onward = (lax.rem(blk + 1, n_blk), group)
    diagonal = (lax.rem(blk + n_blk - 1 + 2 * lax.rem(blk, 2), n_blk), group)
    higher = (blk, lax.rem(group + 1, n_group))
    lower = (blk, lax.rem(group + n_group - 1, n_group))

    load_text = pltpu.make_async_copy(text_hbm, text_ref, load_sem.at[0])
    load_image = pltpu.make_async_copy(image_hbm, image_ref, load_sem.at[1])
    load_text_lse = pltpu.make_async_copy(text_lse_hbm, text_lse_ref, load_sem.at[2])
    load_image_lse = pltpu.make_async_copy(image_lse_hbm, image_lse_ref, load_sem.at[3])
    for load in (load_image, load_text, load_text_lse, load_image_lse):
        load.start()

    barrier = pltpu.get_barrier_semaphore()
    for device in (ahead, behind, partner, diagonal, higher, lower):
        pl.semaphore_signal(barrier, inc=1, device_id=device, device_id_type=MESH)
    pl.semaphore_wait(barrier, 6)

    def part(k):
        return pl.ds(pl.multiple_of(k * chunk, chunk), chunk)

    def piece(j):
        size = rows // PIECES
        return pl.ds(pl.multiple_of(j * size, size), size)

    def copy(src, dst, kind, slot, device):
        return pltpu.make_async_remote_copy(
            src_ref=src, dst_ref=dst, send_sem=send_sem.at[kind, slot], recv_sem=recv_sem.at[kind, slot],
            device_id=device, device_id_type=MESH,
        )

    def to_far(k):
        return copy(text_hbm.at[piece(k)], raw_far.at[piece(k)], TO_FAR, k, ahead)

    def to_mid(k, source):
        return copy(source.at[piece(k)], raw_mid.at[piece(k)], TO_MID, k, partner)

    def lse_to_far():
        return copy(text_lse_hbm, lse_far, TO_FAR, PIECES, ahead)

    def to_mid_direct(j):
        return copy(text_hbm.at[piece(j)], raw_mid.at[piece(j)], TO_MID, j, onward)

    def lse_to_mid():
        return copy(text_lse_hbm, lse_mid, TO_MID, PIECES, onward)

    def to_image():
        return copy(image_hbm, raw_image, TO_IMAGE, 0, lower)

    def lse_to_image():
        return copy(image_lse_hbm, lse_image, TO_IMAGE, PIECES, lower)

    def back_far(k):
        return copy(g_far.at[piece(k)], got_far.at[piece(k)], BACK_FAR, k, behind)

    def back_mid(k):
        return copy(g_mid.at[piece(k)], got_mid.at[piece(k)], BACK_MID, k, partner)

    def back_image():
        return copy(g_image.at[pl.ds(rows, rows)], got_image, BACK_IMAGE, 0, higher)

    lse_to_far().start()
    lse_to_mid().start()
    lse_to_image().start()
    for j in range(DIRECT):
        to_mid_direct(j).start()
    for j in range(PIECES):
        to_far(j).start()

        if j >= DIRECT:
            @pl.when(even)
            def _():
                to_mid(j, text_hbm).start()

        if j == 0:
            to_image().start()

    def take_text(which, raw, k):
        unit, _ = unit_rows(raw[part(k), :])
        text_high[which, part(k), :], text_low[which, part(k), :] = split(unit)

    def take_column(which, lse):
        text_column[which] = jnp.transpose(jnp.broadcast_to(lse[...], (128, rows)))

    def take_image(first, raw):
        @pl.loop(0, CHUNKS)
        def _(k):
            unit, _ = unit_rows(raw[part(k), :])
            here = pl.ds(pl.multiple_of(first + k * chunk, chunk), chunk)
            image_high[here, :], image_low[here, :] = split(unit)

    def tile(which, here, columns, lse, diagonal=False):
        text = (text_high[which, here, :], text_low[which, here, :])
        image = (image_high[columns, :], image_low[columns, :])
        scores = logit_scale * dot_split(text, image, NT)
        weight = (0.5 * logit_scale) * (
            jnp.exp(scores - lse) + jnp.exp(scores - text_column[which, here, 0:1])
        )
        if diagonal:
            row = lax.broadcasted_iota(jnp.int32, weight.shape, 0)
            column = lax.broadcasted_iota(jnp.int32, weight.shape, 1)
            weight = weight - jnp.where(row == column, logit_scale, 0.0)
        weights[which, here, columns] = weight
        return dot_split(split(weight), image, NN)

    first, second, both = pl.ds(0, rows), pl.ds(rows, rows), pl.ds(0, 2 * rows)

    def image_grad(half):
        turned = jnp.concatenate([jnp.transpose(weights[which, :, half]) for which in range(3)], axis=1)
        texts = [ref[...].reshape(3 * rows, width) for ref in (text_high, text_low)]
        return dot_split(split(turned), texts, NN)

    load_image.wait()
    take_image(0, image_ref)
    load_text_lse.wait()
    load_image_lse.wait()
    take_column(OWN, text_lse_ref)
    load_text.wait()

    @pl.loop(0, CHUNKS)
    def _(k):
        take_text(OWN, text_ref, k)

    g_own[...] = tile(OWN, first, first, image_lse_ref[...], diagonal=True)

    lse_to_far().wait_recv()

    take_column(FAR, lse_far)

    def receive_far(j):
        @pl.when(odd)
        def _():
            to_far(j).wait_recv()
            if isinstance(j, int) and j < DIRECT:
                return
            to_mid(j, raw_far).start()

    for j in range(PIECES // 2 - 1):
        receive_far(j)
    lse_to_image().wait_recv()
    to_image().wait_recv()
    take_image(rows, raw_image)

    receive_far(PIECES // 2 - 1)
    g_own[...] += tile(OWN, first, second, lse_image[...])
    receive_far(PIECES // 2)

    lse_to_mid().wait_recv()
    take_column(MID, lse_mid)
    both_lse = jnp.concatenate([image_lse_ref[...], lse_image[...]], axis=1)

    def pass_on(j):
        @pl.when(odd)
        def _():
            back_mid(j).wait_recv()
            g_far[piece(j), :] += got_mid[piece(j), :]
            back_far(j).start()

    half = PIECES // 2

    def receive_last(j):
        @pl.when(j < PIECES)
        def _():
            receive_far(j)

    per = PIECES // CHUNKS

    @pl.loop(0, CHUNKS)
    def _(k):
        late = k >= CHUNKS // 2
        early = k < CHUNKS // 2

        @pl.when(late)
        def _():
            pass_on(2 * k - half)

        for j in range(per):
            to_mid(per * k + j, text_hbm).wait_recv()
        take_text(MID, raw_mid, k)
        g_mid[part(k), :] = tile(MID, part(k), both, both_lse)

        @pl.when(jnp.logical_or(even, late))
        def _():
            for j in range(per):
                back_mid(per * k + j).start()

        @pl.when(early)
        def _():
            receive_far(half + 1 + 2 * k)

        @pl.when(late)
        def _():
            pass_on(2 * k + 1 - half)

        @pl.when(even)
        def _():
            for j in range(per):
                to_far(per * k + j).wait_recv()

        take_text(FAR, raw_far, k)
        g_far[part(k), :] = tile(FAR, part(k), both, both_lse)

        @pl.when(even)
        def _():
            for j in range(per):
                back_far(per * k + j).start()

        @pl.when(early)
        def _():
            receive_last(half + 2 + 2 * k)

        @pl.when(jnp.logical_and(odd, k == CHUNKS // 2 - 1))
        def _():
            for j in range(half):
                back_mid(j).start()

    pass_on(half)
    g_image[second, :] = image_grad(second)
    back_image().start()
    pass_on(half + 1)
    g_image[first, :] = image_grad(first)
    pass_on(half + 2)
    pass_on(half + 3)
    back_image().wait_recv()

    @pl.loop(0, CHUNKS)
    def _(k):
        grad_image_ref[part(k), :] = project_back(
            g_image[part(k), :] + got_image[part(k), :], image_ref[part(k), :]
        )

    @pl.loop(0, CHUNKS)
    def _(k):
        @pl.when(even)
        def _():
            for j in range(per):
                back_mid(per * k + j).wait_recv()
            g_own[part(k), :] += got_mid[part(k), :]

        for j in range(per):
            back_far(per * k + j).wait_recv()
        grad_text_ref[part(k), :] = project_back(
            g_own[part(k), :] + got_far[part(k), :], text_ref[part(k), :]
        )

    lse_to_far().wait_send()
    lse_to_mid().wait_send()
    lse_to_image().wait_send()
    to_image().wait_send()
    back_image().wait_send()

    @pl.loop(0, PIECES)
    def _(k):
        to_far(k).wait_send()
        to_mid(k, text_hbm).wait_send()
        back_far(k).wait_send()
        back_mid(k).wait_send()


def solution(mesh):
    n_blk, n_group = mesh.shape["blk"], mesh.shape["group"]

    def per_device(image_embed, text_embed, image_lse, text_lse):
        rows, width = image_embed.shape
        block = jax.ShapeDtypeStruct((rows, width), jnp.float32)
        whole = pltpu.VMEM((rows, width), jnp.float32)
        line = pltpu.VMEM((1, rows), jnp.float32)
        grads = pl.pallas_call(
            functools.partial(kernel, n_blk, n_group),
            out_shape=(whole, whole),
            in_specs=[pl.BlockSpec(memory_space=pl.ANY)] * 4,
            out_specs=[pl.BlockSpec(memory_space=pltpu.VMEM)] * 2,
            scratch_shapes=[
                whole, whole, line, line, pltpu.SemaphoreType.DMA((4,)),
                whole, whole, whole, line, line, line,
                pltpu.VMEM((3, rows, width), jnp.bfloat16),
                pltpu.VMEM((3, rows, width), jnp.bfloat16),
                pltpu.VMEM((3, rows, 128), jnp.float32),
                pltpu.VMEM((2 * rows, width), jnp.bfloat16),
                pltpu.VMEM((2 * rows, width), jnp.bfloat16),
                pltpu.VMEM((3, rows, 2 * rows), jnp.float32),
                whole, whole, whole, whole, whole,
                pltpu.VMEM((2 * rows, width), jnp.float32),
                whole,
                pltpu.SemaphoreType.DMA((6, PIECES + 1)),
                pltpu.SemaphoreType.DMA((6, PIECES + 1)),
            ],
            compiler_params=pltpu.CompilerParams(
                collective_id=0, has_side_effects=True, vmem_limit_bytes=62 * 1024 * 1024
            ),
        )(image_embed, text_embed, image_lse.reshape(1, rows), text_lse.reshape(1, rows))
        return grads

    spec = P(("blk", "group"), None)
    line = P(("blk", "group"))
    return jax.shard_map(
        per_device, mesh=mesh, in_specs=(spec, spec, line, line), out_specs=(spec, spec), check_vma=False
    )
```

```python
import functools

import jax
import jax.numpy as jnp
from jax import lax
from jax.experimental import pallas as pl
from jax.experimental.pallas import tpu as pltpu
from jax.sharding import PartitionSpec as P

MESH = pl.DeviceIdType.MESH
CHUNKS = 4
PIECES = 8
DIRECT = 0
OWN, MID, FAR = 0, 1, 2
TO_FAR, TO_MID, TO_IMAGE, BACK_FAR, BACK_MID, BACK_IMAGE = range(6)

logit_scale = 100.0
epsilon = 1e-06
NT = (((1,), (1,)), ((), ()))
NN = (((1,), (0,)), ((), ()))


def split(value):
    high = value.astype(jnp.bfloat16)
    return high, (value - high.astype(jnp.float32)).astype(jnp.bfloat16)


def dot_split(a, b, dims):
    dot = functools.partial(lax.dot_general, dimension_numbers=dims, preferred_element_type=jnp.float32)
    rows = a[0].shape[0]
    by_high = dot(jnp.concatenate(a, axis=0), b[0])
    return by_high[:rows] + (by_high[rows:] + dot(a[0], b[1]))


def unit_rows(raw):
    inverse = lax.rsqrt(jnp.sum(raw * raw, axis=-1, keepdims=True) + epsilon)
    return raw * inverse, inverse


def project_back(grad_unit, raw):
    unit, inverse = unit_rows(raw)
    return (grad_unit - unit * jnp.sum(unit * grad_unit, axis=-1, keepdims=True)) * inverse


def kernel(
    n_blk, n_group,
    image_hbm, text_hbm, image_lse_hbm, text_lse_hbm, grad_image_ref, grad_text_ref,
    image_ref, text_ref, image_lse_ref, text_lse_ref, load_sem,
    raw_far, raw_mid, raw_image, lse_far, lse_mid, lse_image,
    text_high, text_low, text_column, image_high, image_low, weights,
    g_own, g_far, g_mid, got_far, got_mid, g_image, got_image,
    send_sem, recv_sem,
):
    rows, width = image_ref.shape
    chunk = rows // CHUNKS
    blk, group = lax.axis_index("blk"), lax.axis_index("group")
    odd = lax.rem(blk, 2) == 1
    even = lax.rem(blk, 2) == 0
    ahead = (lax.rem(blk + 2, n_blk), group)
    behind = (lax.rem(blk + n_blk - 2, n_blk), group)
    partner = (blk + 1 - 2 * lax.rem(blk, 2), group)
    onward = (lax.rem(blk + 1, n_blk), group)
    diagonal = (lax.rem(blk + n_blk - 1 + 2 * lax.rem(blk, 2), n_blk), group)
    higher = (blk, lax.rem(group + 1, n_group))
    lower = (blk, lax.rem(group + n_group - 1, n_group))

    load_text = pltpu.make_async_copy(text_hbm, text_ref, load_sem.at[0])
    load_image = pltpu.make_async_copy(image_hbm, image_ref, load_sem.at[1])
    load_text_lse = pltpu.make_async_copy(text_lse_hbm, text_lse_ref, load_sem.at[2])
    load_image_lse = pltpu.make_async_copy(image_lse_hbm, image_lse_ref, load_sem.at[3])
    for load in (load_image, load_text, load_text_lse, load_image_lse):
        load.start()

    barrier = pltpu.get_barrier_semaphore()
    for device in (ahead, behind, partner, diagonal, higher, lower):
        pl.semaphore_signal(barrier, inc=1, device_id=device, device_id_type=MESH)
    pl.semaphore_wait(barrier, 6)

    def part(k):
        return pl.ds(pl.multiple_of(k * chunk, chunk), chunk)

    def piece(j):
        size = rows // PIECES
        return pl.ds(pl.multiple_of(j * size, size), size)

    def copy(src, dst, kind, slot, device):
        return pltpu.make_async_remote_copy(
            src_ref=src, dst_ref=dst, send_sem=send_sem.at[kind, slot], recv_sem=recv_sem.at[kind, slot],
            device_id=device, device_id_type=MESH,
        )

    def to_far(k):
        return copy(text_hbm.at[piece(k)], raw_far.at[piece(k)], TO_FAR, k, ahead)

    def to_mid(k, source):
        return copy(source.at[piece(k)], raw_mid.at[piece(k)], TO_MID, k, partner)

    def lse_to_far():
        return copy(text_lse_hbm, lse_far, TO_FAR, PIECES, ahead)

    def to_mid_direct(j):
        return copy(text_hbm.at[piece(j)], raw_mid.at[piece(j)], TO_MID, j, onward)

    def lse_to_mid():
        return copy(text_lse_hbm, lse_mid, TO_MID, PIECES, onward)

    def to_image():
        return copy(image_hbm, raw_image, TO_IMAGE, 0, lower)

    def lse_to_image():
        return copy(image_lse_hbm, lse_image, TO_IMAGE, PIECES, lower)

    def back_far(k):
        return copy(g_far.at[piece(k)], got_far.at[piece(k)], BACK_FAR, k, behind)

    def back_mid(k):
        return copy(g_mid.at[piece(k)], got_mid.at[piece(k)], BACK_MID, k, partner)

    def back_image():
        return copy(g_image.at[pl.ds(rows, rows)], got_image, BACK_IMAGE, 0, higher)

    for j in range(DIRECT):
        to_mid_direct(j).start()
    for j in range(PIECES):
        to_far(j).start()

        if j >= DIRECT:
            @pl.when(even)
            def _():
                to_mid(j, text_hbm).start()

        if j == 0:
            to_image().start()
            lse_to_far().start()
            lse_to_mid().start()
            lse_to_image().start()

    def take_text(which, raw, k):
        unit, _ = unit_rows(raw[part(k), :])
        text_high[which, part(k), :], text_low[which, part(k), :] = split(unit)

    def take_column(which, lse):
        text_column[which] = jnp.transpose(jnp.broadcast_to(lse[...], (128, rows)))

    def take_image(first, raw):
        @pl.loop(0, CHUNKS)
        def _(k):
            unit, _ = unit_rows(raw[part(k), :])
            here = pl.ds(pl.multiple_of(first + k * chunk, chunk), chunk)
            image_high[here, :], image_low[here, :] = split(unit)

    def tile(which, here, columns, lse, diagonal=False):
        text = (text_high[which, here, :], text_low[which, here, :])
        image = (image_high[columns, :], image_low[columns, :])
        scores = logit_scale * dot_split(text, image, NT)
        weight = (0.5 * logit_scale) * (
            jnp.exp(scores - lse) + jnp.exp(scores - text_column[which, here, 0:1])
        )
        if diagonal:
            row = lax.broadcasted_iota(jnp.int32, weight.shape, 0)
            column = lax.broadcasted_iota(jnp.int32, weight.shape, 1)
            weight = weight - jnp.where(row == column, logit_scale, 0.0)
        weights[which, here, columns] = weight
        return dot_split(split(weight), image, NN)

    first, second, both = pl.ds(0, rows), pl.ds(rows, rows), pl.ds(0, 2 * rows)

    def image_grad(half):
        turned = jnp.concatenate([jnp.transpose(weights[which, :, half]) for which in range(3)], axis=1)
        texts = [ref[...].reshape(3 * rows, width) for ref in (text_high, text_low)]
        return dot_split(split(turned), texts, NN)

    load_image.wait()
    take_image(0, image_ref)
    load_text_lse.wait()
    load_image_lse.wait()
    take_column(OWN, text_lse_ref)
    load_text.wait()

    @pl.loop(0, CHUNKS)
    def _(k):
        take_text(OWN, text_ref, k)

    g_own[...] = tile(OWN, first, first, image_lse_ref[...], diagonal=True)

    lse_to_far().wait_recv()

    take_column(FAR, lse_far)

    def receive_far(j):
        @pl.when(odd)
        def _():
            to_far(j).wait_recv()
            if isinstance(j, int) and j < DIRECT:
                return
            to_mid(j, raw_far).start()

    for j in range(PIECES // 2 - 1):
        receive_far(j)
    lse_to_image().wait_recv()
    to_image().wait_recv()
    take_image(rows, raw_image)

    receive_far(PIECES // 2 - 1)
    receive_far(PIECES // 2)

    lse_to_mid().wait_recv()
    take_column(MID, lse_mid)
    both_lse = jnp.concatenate([image_lse_ref[...], lse_image[...]], axis=1)

    def pass_on(j):
        @pl.when(odd)
        def _():
            back_mid(j).wait_recv()
            g_far[piece(j), :] += got_mid[piece(j), :]
            back_far(j).start()

    half = PIECES // 2

    def receive_last(j):
        @pl.when(j < PIECES)
        def _():
            receive_far(j)

    per = PIECES // CHUNKS

    @pl.loop(0, CHUNKS)
    def _(k):
        late = k >= CHUNKS // 2
        early = k < CHUNKS // 2

        @pl.when(late)
        def _():
            pass_on(2 * k - half)

        for j in range(per):
            to_mid(per * k + j, text_hbm).wait_recv()
        take_text(MID, raw_mid, k)
        g_mid[part(k), :] = tile(MID, part(k), both, both_lse)

        @pl.when(jnp.logical_or(even, late))
        def _():
            for j in range(per):
                back_mid(per * k + j).start()

        @pl.when(early)
        def _():
            receive_far(half + 1 + 2 * k)

        @pl.when(late)
        def _():
            pass_on(2 * k + 1 - half)

        @pl.when(even)
        def _():
            for j in range(per):
                to_far(per * k + j).wait_recv()

        take_text(FAR, raw_far, k)
        g_far[part(k), :] = tile(FAR, part(k), both, both_lse)

        @pl.when(even)
        def _():
            for j in range(per):
                back_far(per * k + j).start()

        @pl.when(early)
        def _():
            receive_last(half + 2 + 2 * k)

        @pl.when(jnp.logical_and(odd, k == CHUNKS // 2 - 1))
        def _():
            for j in range(half):
                back_mid(j).start()

    g_own[...] += tile(OWN, first, second, lse_image[...])

    pass_on(half)
    g_image[second, :] = image_grad(second)
    back_image().start()
    pass_on(half + 1)
    g_image[first, :] = image_grad(first)
    pass_on(half + 2)
    pass_on(half + 3)
    back_image().wait_recv()

    @pl.loop(0, CHUNKS)
    def _(k):
        grad_image_ref[part(k), :] = project_back(
            g_image[part(k), :] + got_image[part(k), :], image_ref[part(k), :]
        )

    @pl.loop(0, CHUNKS)
    def _(k):
        @pl.when(even)
        def _():
            for j in range(per):
                back_mid(per * k + j).wait_recv()
            g_own[part(k), :] += got_mid[part(k), :]

        for j in range(per):
            back_far(per * k + j).wait_recv()
        grad_text_ref[part(k), :] = project_back(
            g_own[part(k), :] + got_far[part(k), :], text_ref[part(k), :]
        )

    lse_to_far().wait_send()
    lse_to_mid().wait_send()
    lse_to_image().wait_send()
    to_image().wait_send()
    back_image().wait_send()

    @pl.loop(0, PIECES)
    def _(k):
        to_far(k).wait_send()
        to_mid(k, text_hbm).wait_send()
        back_far(k).wait_send()
        back_mid(k).wait_send()


def solution(mesh):
    n_blk, n_group = mesh.shape["blk"], mesh.shape["group"]

    def per_device(image_embed, text_embed, image_lse, text_lse):
        rows, width = image_embed.shape
        block = jax.ShapeDtypeStruct((rows, width), jnp.float32)
        whole = pltpu.VMEM((rows, width), jnp.float32)
        line = pltpu.VMEM((1, rows), jnp.float32)
        grads = pl.pallas_call(
            functools.partial(kernel, n_blk, n_group),
            out_shape=(whole, whole),
            in_specs=[pl.BlockSpec(memory_space=pl.ANY)] * 4,
            out_specs=[pl.BlockSpec(memory_space=pltpu.VMEM)] * 2,
            scratch_shapes=[
                whole, whole, line, line, pltpu.SemaphoreType.DMA((4,)),
                whole, whole, whole, line, line, line,
                pltpu.VMEM((3, rows, width), jnp.bfloat16),
                pltpu.VMEM((3, rows, width), jnp.bfloat16),
                pltpu.VMEM((3, rows, 128), jnp.float32),
                pltpu.VMEM((2 * rows, width), jnp.bfloat16),
                pltpu.VMEM((2 * rows, width), jnp.bfloat16),
                pltpu.VMEM((3, rows, 2 * rows), jnp.float32),
                whole, whole, whole, whole, whole,
                pltpu.VMEM((2 * rows, width), jnp.float32),
                whole,
                pltpu.SemaphoreType.DMA((6, PIECES + 1)),
                pltpu.SemaphoreType.DMA((6, PIECES + 1)),
            ],
            compiler_params=pltpu.CompilerParams(
                collective_id=0, has_side_effects=True, vmem_limit_bytes=62 * 1024 * 1024
            ),
        )(image_embed, text_embed, image_lse.reshape(1, rows), text_lse.reshape(1, rows))
        return grads

    spec = P(("blk", "group"), None)
    line = P(("blk", "group"))
    return jax.shard_map(
        per_device, mesh=mesh, in_specs=(spec, spec, line, line), out_specs=(spec, spec), check_vma=False
    )
```
